256 devices in a mesh: outer: 8 (over x, z_hi), inner: 32 (over z_lo, y, core).
Axes of the slice: x: 4, y: 4, z: 8 (z_hi: 2, z_lo: 4; z = z_hi * 4 + z_lo), core: 2. Of those that a mesh axis runs over, the one named last changes fastest.
Arguments:
- queries: bfloat16 [65536, 1024], P(('outer', 'inner')), may hold values from -5 to 5
- key_rows: bfloat16 [65536, 128], P(('outer', 'inner')), may hold values from -5 to 5
- value_rows: bfloat16 [65536, 128], P(('outer', 'inner')), may hold values from -6 to 6
- grad_out: bfloat16 [65536, 1024], P(('outer', 'inner')), may hold values from -12 to 12
- doc_ids: int32 [65536], P(('outer', 'inner')), may hold values from 0 to 63, never falling along the last dimension, each value on 1 to 2048 neighbouring positions
Outputs:
- grad_queries: bfloat16 [65536, 1024], P(('outer', 'inner'))
- grad_keys: bfloat16 [65536, 128], P(('outer', 'inner'))
- grad_values: bfloat16 [65536, 128], P(('outer', 'inner'))
The draws below stay inside these ranges and needn't reach their ends.
Inputs may be any that keep to these rules, and one draw needn't show every extreme that they name: `doc_ids`: ids never fall along the tokens; each document holds at most 2048 consecutive tokens and some document holds exactly 2048.
All inputs are finite; a program needn't handle non-finite values.
Results may differ from the reference program's by a relative error of at most 0.011.
Values may be sent and summed in bfloat16 or wider, within the bound.
No kernel may reach another device: no remote copies, remote signals or barrier semaphores. Data moves between devices by JAX's collectives and lax.ppermute only.
A program may use at most 128 MiB of HBM per device.

```python
import math
import jax
import jax.numpy as jnp
import numpy as np
from jax import lax

H = 8
DH = 128
TOK_DEV = 256
MAXDOC = 2048
REACH = 8
TOKENS = 65536
DOCS = 64


def draw_queries(key, part):
    key = jax.random.fold_in(key, 11)
    drawn = jnp.clip(jax.random.normal(key, (TOKENS, H * DH), jnp.float32), -4.5, 4.5)
    return drawn.astype(jnp.bfloat16)


def draw_key_rows(key, part):
    key = jax.random.fold_in(key, 12)
    drawn = jnp.clip(jax.random.normal(key, (TOKENS, DH), jnp.float32), -4.5, 4.5)
    return drawn.astype(jnp.bfloat16)


def shard_levels(key, extent, pieces, least, largest):
    gain = 1.0
    for axis_at, shards_of in pieces:
        heights = jax.random.uniform(jax.random.fold_in(jax.random.fold_in(key, 6), axis_at), (shards_of,), jnp.float32, least / len(pieces), largest / len(pieces))
        gain = gain * jnp.repeat(jnp.exp(heights), extent[axis_at] // shards_of).reshape((-1,) + (1,) * (len(extent) - 1 - axis_at))
    return gain


def profile(number_of, total, most, slope):
    loads = [(1 << 20) // math.isqrt(grade ** slope) + 1 for grade in range(2, number_of + 1)]
    rest, given = total - most - (number_of - 1), [1] * (number_of - 1)
    while rest > 0:
        movable = [i for i in range(number_of - 1) if given[i] < most]
        pool, budget = sum([loads[i] for i in movable]), rest
        for i in movable:
            addition = min(most - given[i], max(1, budget * loads[i] // pool), rest)
            given[i] = given[i] + addition
            rest = rest - addition
    return np.array([most] + given)


def uneven(own_key, count, total, most, skew):
    if count == 2:
        one = jax.random.randint(own_key, (), max(1, total - most), min(most, total - 1) + 1)
        return jnp.stack([one, total - one])
    sizes = jnp.asarray(profile(count, total, most, skew), jnp.int32)
    couples = (count - 1) // 2
    source_of, taker = sizes[1:1 + 2 * couples:2], sizes[2:2 + 2 * couples:2]
    room = jnp.minimum(source_of - 1, most - taker)
    moved = jax.random.randint(jax.random.fold_in(own_key, 1), (couples,), 0, 1 << 20) % (room + 1)
    sizes = sizes.at[1:1 + 2 * couples:2].set(source_of - moved).at[2:2 + 2 * couples:2].set(taker + moved)
    return sizes[jax.random.permutation(jax.random.fold_in(own_key, 2), count)]


def bell_draw(rng, shape, width, bound, pieces=(), kind=jnp.bfloat16):
    array = width * jax.random.normal(rng, shape, jnp.float32)
    if pieces:
        array = array * shard_levels(rng, shape, pieces, -0.22, 0.18)
    return jnp.clip(array, -bound, bound).astype(kind)


def setup_inputs(seed: int = 0) -> dict:
    streams_of = jax.random.split(jax.random.key(seed), 6)
    queries = draw_queries(jax.random.fold_in(streams_of[5], 71), 0)
    key_rows = draw_key_rows(jax.random.fold_in(streams_of[5], 71), 0)
    value_rows = bell_draw(streams_of[2], (TOKENS, DH), 1.0, 6.0, ((0, 256),))
    grad_out = bell_draw(streams_of[3], (TOKENS, H * DH), 2.0, 12.0, ((0, 256),))
    doc_ids = jnp.searchsorted(jnp.cumsum(uneven(streams_of[4], DOCS, TOKENS, MAXDOC, 0)), jnp.arange(TOKENS), side="right").astype(jnp.int32)
    return {"queries": queries, "key_rows": key_rows, "value_rows": value_rows, "grad_out": grad_out, "doc_ids": doc_ids}


def reference(queries, key_rows, value_rows, grad_out, doc_ids):
    margin = REACH * TOK_DEV
    window = (REACH + 1) * TOK_DEV
    scale = 1.0 / (DH ** 0.5)
    pad_keys = jnp.concatenate([jnp.zeros((margin, DH), key_rows.dtype), key_rows], 0)
    pad_values = jnp.concatenate([jnp.zeros((margin, DH), value_rows.dtype), value_rows], 0)
    pad_ids = jnp.concatenate([jnp.full((margin,), -1, jnp.int32), doc_ids.astype(jnp.int32)], 0)

    def block(carry, index):
        keys_acc, values_acc = carry
        start = (index * TOK_DEV).astype(jnp.int32)
        query_block = lax.dynamic_slice_in_dim(queries, start, TOK_DEV, 0).reshape(TOK_DEV, H, DH).astype(jnp.float32)
        grad_block = lax.dynamic_slice_in_dim(grad_out, start, TOK_DEV, 0).reshape(TOK_DEV, H, DH).astype(jnp.float32)
        block_ids = lax.dynamic_slice_in_dim(doc_ids.astype(jnp.int32), start, TOK_DEV, 0)
        key_win = lax.dynamic_slice_in_dim(pad_keys, start, window, 0).astype(jnp.float32)
        value_win = lax.dynamic_slice_in_dim(pad_values, start, window, 0).astype(jnp.float32)
        win_ids = lax.dynamic_slice_in_dim(pad_ids, start, window, 0)
        query_pos = start + jnp.arange(TOK_DEV, dtype=jnp.int32)
        key_pos = start - margin + jnp.arange(window, dtype=jnp.int32)
        allowed = (win_ids[None, :] == block_ids[:, None]) & (key_pos[None, :] <= query_pos[:, None])
        allowed = allowed[None]
        scores = jnp.einsum('thd,wd->htw', query_block, key_win) * scale
        peak = jnp.max(jnp.where(allowed, scores, -jnp.inf), axis=2, keepdims=True)
        expo = jnp.where(allowed, jnp.exp(scores - peak), 0.0)
        total = jnp.sum(expo, axis=2, keepdims=True)
        probs = expo / total
        probs_half = probs.astype(jnp.bfloat16).astype(jnp.float32)
        output = jnp.einsum('htw,wd->thd', probs_half, value_win)
        delta = jnp.sum(grad_block * output, axis=2)
        grad_probs = jnp.einsum('thd,wd->htw', grad_block, value_win)
        grad_scores = (probs * (grad_probs - delta.T[:, :, None]) * scale).astype(jnp.bfloat16).astype(jnp.float32)
        grad_query = jnp.einsum('htw,wd->thd', grad_scores, key_win).reshape(TOK_DEV, H * DH).astype(jnp.bfloat16)
        grad_key_win = jnp.einsum('htw,thd->wd', grad_scores, query_block)
        grad_value_win = jnp.einsum('htw,thd->wd', probs_half, grad_block)
        keys_new = lax.dynamic_slice_in_dim(keys_acc, start, window, 0) + grad_key_win
        values_new = lax.dynamic_slice_in_dim(values_acc, start, window, 0) + grad_value_win
        keys_acc = lax.dynamic_update_slice_in_dim(keys_acc, keys_new, start, 0)
        values_acc = lax.dynamic_update_slice_in_dim(values_acc, values_new, start, 0)
        return (keys_acc, values_acc), grad_query

    initial = (jnp.zeros((margin + TOKENS, DH), jnp.float32), jnp.zeros((margin + TOKENS, DH), jnp.float32))
    (keys_acc, values_acc), grad_queries = lax.scan(block, initial, jnp.arange(TOKENS // TOK_DEV, dtype=jnp.int32))
    return (grad_queries.reshape(TOKENS, H * DH), keys_acc[margin:].astype(jnp.bfloat16), values_acc[margin:].astype(jnp.bfloat16))
```

```python
import functools
import jax, jax.numpy as jnp
from jax import lax
from jax.sharding import PartitionSpec as P_
from jax.experimental import pallas as pl
from jax.experimental.pallas import tpu as pltpu
DH=128; B=256; MR=528; H=8
C=float(1.0/DH**0.5*1.4426950408889634)
SC=float(1.0/DH**0.5)
NEG=-1e30
f32=jnp.float32; bf16=jnp.bfloat16
VM=pl.BlockSpec(memory_space=pltpu.VMEM)
SM=pl.BlockSpec(memory_space=pltpu.SMEM)
def dot(a,b): return jnp.dot(a,b,preferred_element_type=f32)
def vin(x): return pltpu.with_memory_space_constraint(x,pltpu.VMEM)
def vout(shape,dt): return pltpu.VMEM(shape,dt)

def classify(parity,steps,rows,kvs,cls,cnt):
    for n,s in enumerate(steps):
        ids=kvs[n][pl.ds(2*B,16),:].astype(f32)[0:2]
        for b in range(2):
            r=rows[b][0:1,:]
            lo=jnp.min(r); hi=jnp.max(r)
            match=jnp.sum(jnp.where(ids==lo,1.0,0.0)).astype(jnp.int32)
            t=2*n+b
            if s==0 and b==0:
                cls[t]=1; cnt[t]=0
            else:
                some=match>0
                if s==0: some=some&(parity==0)
                cls[t]=jnp.where(some,jnp.where((match==B)&(lo==hi),2,1),0)
                cnt[t]=B-match
def bias_of(diag,r,cnt):
    tpos=lax.broadcasted_iota(jnp.int32,(1,B),1).astype(f32)
    if diag: lb=r[1:2]; ub=tpos
    else: lb=jnp.where(r[2:3]>0.5,cnt.astype(f32),1e9); ub=None
    u=lax.broadcasted_iota(jnp.int32,(B,B),0).astype(f32)
    ok=(u>=lb)
    if diag: ok=ok&(u<=ub)
    return jnp.where(ok,0.0,NEG)

def p1_kernel(steps,first,*refs):
    n_kv=len(steps)
    it=iter(refs)
    sc=next(it); rows=[next(it),next(it)]
    if first: qd=[next(it) for _ in range(4)]
    else: qt,dt=next(it),next(it)
    kvs=[next(it) for _ in range(n_kv)]
    if not first: st_in=next(it)
    st=next(it); P=next(it); D=next(it); mj=next(it)
    if first: qt,dt=next(it),next(it)
    cls,cnt=next(it),next(it)
    if first:
        for b in range(2):
            for h in range(H):
                sl=pl.ds(h*DH,DH)
                qt[b*H+h]=qd[b][:,sl].T
                dt[b*H+h]=qd[2+b][:,sl].T
                st[b*H+h]=jnp.concatenate([jnp.full((1,B),NEG,f32),jnp.zeros((7,B),f32)],0)
    else: st[...]=st_in[...]
    classify(sc[0],steps,rows,kvs,cls,cnt)
    def tile(n,b,masked):
        t=2*n+b
        K=kvs[n][pl.ds(0,B),:]; V=kvs[n][pl.ds(B,B),:]
        if masked: bias=bias_of(steps[n]==0 and b==0,rows[b],cnt[t])
        def head(h,_):
            S=dot(K,qt[b*H+h])
            if masked: S=S+bias
            old=st[b*H+h]
            mn=jnp.maximum(old[0:1],jnp.max(S,axis=0,keepdims=True))
            p=jnp.exp2(S*C-mn*C)
            dP=dot(V,dt[b*H+h])
            al=jnp.exp2((old[0:1]-mn)*C)
            l=old[1:2]*al+jnp.sum(p,axis=0,keepdims=True)
            d=old[2:3]*al+jnp.sum(p*dP,axis=0,keepdims=True)
            st[b*H+h,0:1]=mn; st[b*H+h,1:2]=l; st[b*H+h,2:3]=d
            mj[t*H+h,0:1]=mn
            P[t*H+h]=p.astype(bf16)
            D[t*H+h]=dP
            return 0
        for h in range(H): head(h,0)
    for n in range(n_kv):
        for b in range(2):
            c=cls[2*n+b]
            @pl.when(c==1)
            def _(): tile(n,b,True)
            if not (steps[n]==0 and b==0):
                @pl.when(c==2)
                def _(): tile(n,b,False)
def p1(steps,sc,rows,ops,kvs,st=None):
    n=len(steps); first=st is None
    outs=[vout((2*H,8,B),f32),vout((2*n*H,B,B),bf16),vout((2*n*H,B,B),f32),vout((2*n*H,8,B),f32)]
    if first: outs+=[vout((2*H,DH,B),bf16)]*2
    args=[*rows,*ops,*kvs]+([] if first else [st])
    return pl.pallas_call(functools.partial(p1_kernel,steps,first),
      out_shape=tuple(outs),
      in_specs=[SM]+[VM]*len(args), out_specs=tuple([VM]*len(outs)),
      scratch_shapes=[pltpu.SMEM((2*n,),jnp.int32),pltpu.SMEM((2*n,),jnp.int32)],
      compiler_params=pltpu.CompilerParams(vmem_limit_bytes=8*2**20),name="scores_"+"".join(map(str,steps)))(sc,*[vin(a) for a in args])

def p2_kernel(steps,take,first,last,*refs):
    n_kv=len(steps)
    it=iter(refs)
    sc=next(it); rows=[next(it),next(it)]; qs=[next(it),next(it)]; dos=[next(it),next(it)]
    sta,stb=next(it),next(it); P,D,mj=next(it),next(it),next(it)
    kvs=[next(it) for _ in range(n_kv)]
    if not first: dq_in=next(it)
    gs=[next(it) for _ in range(n_kv)]
    if last: dqo,dqp=next(it),next(it)
    else: dq=next(it)
    cls,cnt,L,acc=next(it),next(it),next(it),next(it)
    if last: dq=dq_in if not first else next(it)
    if first: dq[...]=jnp.zeros_like(dq)
    for b in range(2):
        for h in range(H):
            x=sta[b*H+h]; y=stb[(1-b)*H+h]
            m=jnp.maximum(x[0:1],y[0:1])
            ax=jnp.exp2((x[0:1]-m)*C); ay=jnp.exp2((y[0:1]-m)*C)
            l=x[1:2]*ax+y[1:2]*ay
            L[b*H+h,0:1]=m*C+jnp.log2(l)
            L[b*H+h,1:2]=(x[2:3]*ax+y[2:3]*ay)/l
    classify(sc[0],steps,rows,kvs,cls,cnt)
    for n in range(n_kv):
        acc[...]=jnp.zeros_like(acc)
        K=kvs[n][pl.ds(0,B),:]
        Kt=K.T
        for b in range(2):
            @pl.when(cls[2*n+b]>0)
            def _():
                t=2*take[n]+b
                dk=jnp.zeros((B,DH),f32); dv=jnp.zeros((B,DH),f32)
                for h in range(H):
                    sl=pl.ds(h*DH,DH)
                    fac=jnp.exp2(mj[t*H+h,0:1]*C-L[b*H+h,0:1])
                    p=P[t*H+h].astype(f32)*fac
                    g=(p*(D[t*H+h]-L[b*H+h,1:2])).astype(bf16)
                    dv=dv+dot(p.astype(bf16),dos[b][:,sl])
                    dk=dk+dot(g,qs[b][:,sl])
                    dq[b*H+h]+=dot(Kt,g)
                acc[0]+=dk; acc[1]+=dv
        gs[n][pl.ds(0,B),:]=(acc[0]*SC).astype(bf16)
        gs[n][pl.ds(B,B),:]=acc[1].astype(bf16)
    if last:
        for h in range(H):
            sl=pl.ds(h*DH,DH)
            dqo[:,sl]=dq[h].T*SC
            dqp[:,sl]=(dq[H+h].T*SC).astype(bf16)
def p2(steps,take,sc,rows,qs,dos,sta,stb,pdm,kvs,dq=None,last=False):
    n=len(steps); first=dq is None
    outs=[vout((2*B,DH),bf16)]*n
    if last: outs+=[jax.ShapeDtypeStruct((B,H*DH),f32),jax.ShapeDtypeStruct((B,H*DH),bf16)]
    else: outs+=[vout((2*H,DH,B),f32)]
    args=[*rows,*qs,*dos,sta,stb,*pdm,*kvs]+([] if first else [dq])
    alias={} if first or last else {len(args):n}
    return pl.pallas_call(functools.partial(p2_kernel,steps,take,first,last),
      out_shape=tuple(outs),
      in_specs=[SM]+[VM]*len(args), out_specs=tuple([VM]*len(outs)),
      scratch_shapes=[pltpu.SMEM((2*n,),jnp.int32),pltpu.SMEM((2*n,),jnp.int32),
        pltpu.VMEM((2*H,8,B),f32),pltpu.VMEM((2,B,DH),f32)]+([pltpu.VMEM((2*H,DH,B),f32)] if first and last else []),
      input_output_aliases=alias,
      compiler_params=pltpu.CompilerParams(vmem_limit_bytes=12*2**20),name="grads_"+"".join(map(str,steps)))(sc,*[vin(a) for a in args])

AXES=("outer","inner")
def shift(x,by):
    n=lax.axis_size(AXES)
    return lax.ppermute(x,AXES,[(i,(i+by)%n) for i in range(n)])
def swap(x):
    n=lax.axis_size(AXES)
    return lax.ppermute(x,AXES,[(i,i^1) for i in range(n)])

def body(queries,key_rows,value_rows,grad_out,doc_ids):
    ids=doc_ids.astype(f32)
    packed=jnp.pad(ids.reshape(B//DH,DH),((0,MR-2*B-B//DH),(0,0)),constant_values=-1.0).astype(bf16)
    own=jnp.concatenate([key_rows,value_rows,packed],0)
    row_own=jnp.zeros((8,B),f32)
    begin=jnp.sum((ids[:,None]<ids[None,:]).astype(f32),axis=0)
    row_own=jnp.concatenate([ids[None],begin[None],(ids==ids[0]).astype(f32)[None],jnp.zeros((5,B),f32)],0)
    got={s:shift(own,2*s) for s in (4,3,2,1)}
    row_other=swap(row_own); q_other=swap(queries); do_other=swap(grad_out)
    sc=(lax.axis_index("inner")%2).astype(jnp.int32).reshape(1)
    rows=(row_own,row_other); qs=(queries,q_other); dos=(grad_out,do_other)
    st,P0,D0,m0,qt,dt=p1((0,),sc,rows,(*qs,*dos),[own])
    st,PB,DB,mB=p1((1,2,3,4),sc,rows,(qt,dt),[got[s] for s in (1,2,3,4)],st)
    st2=swap(st)
    back=[]
    g4,g3,dq=p2((4,3),(3,2),sc,rows,qs,dos,st,st2,(PB,DB,mB),(got[4],got[3]))
    back+=[shift(g4,-8),shift(g3,-6)]
    g2,g1,dq=p2((2,1),(1,0),sc,rows,qs,dos,st,st2,(PB,DB,mB),(got[2],got[1]),dq)
    back+=[shift(g2,-4),shift(g1,-2)]
    g0,dq_own,dq_part=p2((0,),(0,),sc,rows,qs,dos,st,st2,(P0,D0,m0),(own,),dq,last=True)
    grad_queries=(dq_own+swap(dq_part).astype(f32)).astype(bf16)
    total=g0.astype(f32)
    for x in back: total=total+x.astype(f32)
    total=total.astype(bf16)
    return grad_queries,total[:B],total[B:]

def solution(mesh):
    spec=P_(AXES,None)
    return jax.shard_map(body,mesh=mesh,in_specs=(spec,spec,spec,spec,P_(AXES)),out_specs=(spec,spec,spec),check_vma=False)
```

```python
import functools
import jax, jax.numpy as jnp
from jax import lax
from jax.sharding import PartitionSpec as P_
from jax.experimental import pallas as pl
from jax.experimental.pallas import tpu as pltpu
DH=128; B=256; MR=528; H=8
C=float(1.0/DH**0.5*1.4426950408889634)
SC=float(1.0/DH**0.5)
NEG=-1e30
f32=jnp.float32; bf16=jnp.bfloat16
VM=pl.BlockSpec(memory_space=pltpu.VMEM)
SM=pl.BlockSpec(memory_space=pltpu.SMEM)
HBM=pl.BlockSpec(memory_space=pltpu.HBM)
SMALL=pl.CostEstimate(flops=1024,bytes_accessed=1024,transcendentals=0)
LARGE=pl.CostEstimate(flops=10**10,bytes_accessed=1024,transcendentals=0)
def dot(a,b): return jnp.dot(a,b,preferred_element_type=f32)
def hbm(x): return pltpu.with_memory_space_constraint(x,pltpu.HBM)
def vin(x): return pltpu.with_memory_space_constraint(x,pltpu.VMEM)
def vout(shape,dt): return pltpu.VMEM(shape,dt)
def loop(n,f,unroll=1):
    def body(i,c):
        f(i)
        return c
    lax.fori_loop(0,n,body,0,unroll=unroll)

def pack_kernel(ids,k,v,msg,row,xi,sem):
    copies=[pltpu.make_async_copy(ids,xi,sem.at[0]),
            pltpu.make_async_copy(k,msg.at[pl.ds(0,B)],sem.at[1]),
            pltpu.make_async_copy(v,msg.at[pl.ds(B,B)],sem.at[2])]
    for c in copies: c.start()
    for c in copies: c.wait()
    x=xi[...].astype(f32)
    msg[pl.ds(2*B,16),:]=jnp.concatenate([x,jnp.full((14,DH),-1.0,f32)],0).astype(bf16)
    r=jnp.concatenate([x[0:1],x[1:2]],1)
    col=jnp.broadcast_to(r,(8,B)).T[:,0:1]
    begin=jnp.sum(jnp.where(col<r,1.0,0.0),axis=0,keepdims=True)
    same=jnp.where(r==jnp.min(r),1.0,0.0)
    row[...]=jnp.concatenate([r,begin,same,jnp.zeros((5,B),f32)],0)
def pack(ids,k,v):
    return pl.pallas_call(pack_kernel,
      out_shape=(vout((MR,DH),bf16),vout((8,B),f32)),
      in_specs=[HBM]*3,out_specs=(VM,VM),name="pack",
      scratch_shapes=[pltpu.VMEM((B//DH,DH),jnp.int32),pltpu.SemaphoreType.DMA((3,))],cost_estimate=SMALL,
      compiler_params=pltpu.CompilerParams(vmem_limit_bytes=4*2**20))(*[hbm(a) for a in (ids.reshape(B//DH,DH),k,v)])

def classify(parity,steps,rows,kv,cls,cnt):
    lo=[jnp.min(r[0:1,:]) for r in rows]
    one=[jnp.min(r[2:3,:])>0.5 for r in rows]
    for n,s in enumerate(steps):
        ids=kv[n,pl.ds(2*B,16),:].astype(f32)[0:2]
        for b in range(2):
            t=2*n+b
            if s==0 and b==0:
                cls[t]=1; cnt[t]=0
            else:
                match=jnp.sum(jnp.where(ids==lo[b],1.0,0.0)).astype(jnp.int32)
                some=match>0
                if s==0: some=some&(parity==0)
                cls[t]=jnp.where(some,jnp.where((match==B)&one[b],2,1),0)
                cnt[t]=B-match
def bias_of(diag,rows,b,cnt):
    begin=jnp.where(b==0,rows[0][1:2],rows[1][1:2]); first=jnp.where(b==0,rows[0][2:3],rows[1][2:3])
    lb=jnp.where(first>0.5,cnt.astype(f32),1e9)
    u=lax.broadcasted_iota(jnp.int32,(B,B),0).astype(f32)
    if diag:
        lb=jnp.where(b==0,begin,lb)
        ub=jnp.where(b==0,lax.broadcasted_iota(jnp.int32,(1,B),1).astype(f32),1e9)
        return jnp.where((u>=lb)&(u<=ub),0.0,NEG)
    return jnp.where(u>=lb,0.0,NEG)

def p1_kernel(steps,first,*refs):
    n_kv=len(steps)
    it=iter(refs)
    sc=next(it); rows=[next(it),next(it)]
    if first: qd=[next(it) for _ in range(4)]
    else: qt,dt=next(it),next(it)
    kvs=[next(it) for _ in range(n_kv)]
    if not first: st_in=next(it)
    st=next(it); P=next(it); D=next(it); mj=next(it)
    if first: qt,dt,qn,dn=next(it),next(it),next(it),next(it)
    cls,cnt,bias=next(it),next(it),next(it)
    kv,sem=next(it),next(it)
    fetch=[pltpu.make_async_copy(kvs[n],kv.at[n],sem.at[2+n]) for n in range(n_kv)]
    for c in fetch: c.start()
    if first:
        qv,dv=next(it),next(it)
        copies=[pltpu.make_async_copy(qd[0],qv,sem.at[0]),pltpu.make_async_copy(qd[2],dv,sem.at[1])]
        for c in copies: c.start()
        def flip(b,q,d):
            for h in range(H):
                x=q[:,pl.ds(h*DH,DH)]; y=d[:,pl.ds(h*DH,DH)]
                qn[b*H+h]=x; dn[b*H+h]=y
                qt[b*H+h]=x.T; dt[b*H+h]=y.T
        flip(1,qd[1],qd[3])
        def clear(i): st[i]=jnp.concatenate([jnp.full((1,B),NEG,f32),jnp.zeros((7,B),f32)],0)
        loop(2*H,clear)
        for c in fetch: c.wait()
        classify(sc[0],steps,rows,kv,cls,cnt)
        for c in copies: c.wait()
        flip(0,qv,dv)
    else:
        st[...]=st_in[...]
        for c in fetch: c.wait()
        classify(sc[0],steps,rows,kv,cls,cnt)
    def tile(t,masked):
        n=t//2; b=t%2
        if masked: bias[...]=bias_of(steps[0]==0,rows,b,cnt[t])
        K=kv[n,pl.ds(0,B),:]; V=kv[n,pl.ds(B,B),:]
        for h in range(H):
            i=b*H+h; j=t*H+h
            S=dot(K,qt[i])
            if masked: S=S+bias[...]
            old=st[i]
            mn=jnp.maximum(old[0:1],jnp.max(S,axis=0,keepdims=True))
            p=jnp.exp2(S*C-mn*C)
            dP=dot(V,dt[i])
            al=jnp.exp2((old[0:1]-mn)*C)
            l=old[1:2]*al+jnp.sum(p,axis=0,keepdims=True)
            d=old[2:3]*al+jnp.sum(p*dP,axis=0,keepdims=True)
            st[i,0:1]=mn; st[i,1:2]=l; st[i,2:3]=d
            mj[j,0:1]=mn
            P[j]=p.astype(bf16)
            D[j]=dP
    def pick(t):
        c=cls[t]
        @pl.when(c==1)
        def _(): tile(t,True)
        @pl.when(c==2)
        def _(): tile(t,False)
    loop(2*n_kv,pick)
def p1(steps,sc,rows,ops,kvs,st=None):
    n=len(steps); first=st is None
    outs=[vout((2*H,8,B),f32),vout((2*n*H,B,B),bf16),vout((2*n*H,B,B),f32),vout((2*n*H,8,B),f32)]
    if first: outs+=[vout((2*H,DH,B),bf16)]*2+[vout((2*H,B,DH),bf16)]*2
    ops=[hbm(ops[0]),vin(ops[1]),hbm(ops[2]),vin(ops[3])] if first else [vin(a) for a in ops]
    args=[*[vin(r) for r in rows],*ops,*[vin(a) for a in kvs]]+([] if first else [vin(st)])
    specs=[SM]+[VM]*len(args)
    if first: specs[3]=specs[5]=HBM
    return pl.pallas_call(functools.partial(p1_kernel,steps,first),
      out_shape=tuple(outs),
      in_specs=specs, out_specs=tuple([VM]*len(outs)),
      scratch_shapes=[pltpu.SMEM((2*n,),jnp.int32),pltpu.SMEM((2*n,),jnp.int32),pltpu.VMEM((B,B),f32),
        pltpu.VMEM((n,MR,DH),bf16),pltpu.SemaphoreType.DMA((2+n,))]+([pltpu.VMEM((B,H*DH),bf16)]*2 if first else []),
      cost_estimate=SMALL,compiler_params=pltpu.CompilerParams(vmem_limit_bytes=6*2**20),name="scores_"+"".join(map(str,steps)))(sc,*args)

def p2_kernel(steps,take,first,last,n_back,*refs):
    n_kv=len(steps)
    it=iter(refs)
    sc=next(it); rows=[next(it),next(it)]; qn=next(it); dn=next(it)
    sta,stb=next(it),next(it); P,D,mj=next(it),next(it),next(it)
    kvs=[next(it) for _ in range(n_kv)]
    if not first: dq_in=next(it)
    back=[next(it) for _ in range(n_back)]
    gs=[next(it) for _ in range(n_kv)]
    if last: dqo,dqp=next(it),next(it)
    else: dq=next(it)
    cls,cnt,L,acc,kv,kt,sem=[next(it) for _ in range(7)]
    fetch=[pltpu.make_async_copy(kvs[n],kv.at[n],sem.at[n]) for n in range(n_kv)]
    for c in fetch: c.start()
    if last: dq=dq_in
    if first: dq[...]=jnp.zeros_like(dq)
    def total(i):
        x=sta[i]; y=stb[(i+H)%(2*H)]
        m=jnp.maximum(x[0:1],y[0:1])
        ax=jnp.exp2((x[0:1]-m)*C); ay=jnp.exp2((y[0:1]-m)*C)
        l=x[1:2]*ax+y[1:2]*ay
        L[i]=jnp.concatenate([m*C+jnp.log2(l),(x[2:3]*ax+y[2:3]*ay)/l,jnp.zeros((6,B),f32)],0)
    loop(2*H,total,2)
    for c in fetch: c.wait()
    classify(sc[0],steps,rows,kv,cls,cnt)
    acc[...]=jnp.zeros_like(acc)
    for n in range(n_kv): kt[n]=kv[n,pl.ds(0,B),:].T
    def pick(t):
        n=t//2; b=t%2
        @pl.when(cls[t]>0)
        def _():
            at=take[0]+n*(take[-1]-take[0])
            dk=jnp.zeros((B,DH),f32); dv=jnp.zeros((B,DH),f32)
            for h in range(H):
                i=b*H+h; j=(2*at+b)*H+h
                fac=jnp.exp2(mj[j,0:1]*C-L[i,0:1])
                p=P[j].astype(f32)*fac
                g=(p*(D[j]-L[i,1:2])).astype(bf16)
                dv=dv+dot(p.astype(bf16),dn[i])
                dk=dk+dot(g,qn[i])
                dq[i]+=dot(kt[n],g)
            acc[n,0]+=dk; acc[n,1]+=dv
    loop(2*n_kv,pick)
    for n in range(n_kv):
        dk=acc[n,0]*SC; dv=acc[n,1]
        if last:
            for x in back:
                dk=dk+x[pl.ds(0,B),:].astype(f32); dv=dv+x[pl.ds(B,B),:].astype(f32)
        gs[n][pl.ds(0,B),:]=dk.astype(gs[n].dtype)
        gs[n][pl.ds(B,B),:]=dv.astype(gs[n].dtype)
    if last:
        for h in range(H):
            sl=pl.ds(h*DH,DH)
            dqo[:,sl]=dq[h].T*SC
            dqp[:,sl]=(dq[H+h].T*SC).astype(bf16)
def p2(steps,take,sc,rows,qn,dn,sta,stb,pdm,kvs,dq=None,last=False,back=()):
    n=len(steps); first=dq is None
    outs=[vout((2*B,DH),f32 if last else bf16)]*n
    if last: outs+=[vout((B,H*DH),f32),vout((B,H*DH),bf16)]
    else: outs+=[vout((2*H,DH,B),f32)]
    args=[*rows,qn,dn,sta,stb,*pdm,*kvs]+([] if first else [dq])
    alias={} if first or last else {len(args):n}
    args+=list(back)
    return pl.pallas_call(functools.partial(p2_kernel,steps,take,first,last,len(back)),
      out_shape=tuple(outs),
      in_specs=[SM]+[VM]*len(args), out_specs=tuple([VM]*len(outs)),
      scratch_shapes=[pltpu.SMEM((2*n,),jnp.int32),pltpu.SMEM((2*n,),jnp.int32),
        pltpu.VMEM((2*H,8,B),f32),pltpu.VMEM((n,2,B,DH),f32),
        pltpu.VMEM((n,MR,DH),bf16),pltpu.VMEM((n,DH,B),bf16),pltpu.SemaphoreType.DMA((n,))],
      input_output_aliases=alias,
      cost_estimate=SMALL if first else LARGE,compiler_params=pltpu.CompilerParams(vmem_limit_bytes=8*2**20),name="grads_"+"".join(map(str,steps)))(sc,*[vin(a) for a in args])

def sum_kernel(t,x,y,dk,dv):
    s=t[...]+x[...].astype(f32)+y[...].astype(f32)
    dk[...]=s[0:B].astype(bf16)
    dv[...]=s[B:].astype(bf16)
def sum_parts(*args):
    o=jax.ShapeDtypeStruct((B,DH),bf16)
    return pl.pallas_call(sum_kernel,out_shape=(o,o),
      in_specs=[VM]*3,out_specs=(VM,VM),name="sum_parts",cost_estimate=LARGE,
      compiler_params=pltpu.CompilerParams(vmem_limit_bytes=8*2**20))(*[vin(a) for a in args])

AXES=("outer","inner")
def shift(x,by):
    n=lax.axis_size(AXES)
    return lax.ppermute(x,AXES,[(i,(i+by)%n) for i in range(n)])
def swap(x):
    n=lax.axis_size(AXES)
    return lax.ppermute(x,AXES,[(i,i^1) for i in range(n)])

def body(queries,key_rows,value_rows,grad_out,doc_ids):
    own,row_own=pack(doc_ids,key_rows,value_rows)
    got={s:shift(own,2*s) for s in (2,4,3,1)}
    row_other=swap(row_own); q_other=swap(queries); do_other=swap(grad_out)
    sc=(lax.axis_index("inner")%2).astype(jnp.int32).reshape(1)
    rows=(row_own,row_other)
    st,P0,D0,m0,qt,dt,qn,dn=p1((0,),sc,rows,(queries,q_other,grad_out,do_other),[own])
    st,*near=p1((1,3),sc,rows,(qt,dt),(got[1],got[3]),st)
    st,*far=p1((4,2),sc,rows,(qt,dt),(got[4],got[2]),st)
    st2=swap(st)
    g4,g2,dq=p2((4,2),(0,1),sc,rows,qn,dn,st,st2,far,(got[4],got[2]))
    back=[shift(g4,-8),shift(g2,-4)]
    g3,g1,dq=p2((3,1),(1,0),sc,rows,qn,dn,st,st2,near,(got[3],got[1]),dq)
    late=[shift(g3,-6),shift(g1,-2)]
    total,dq_own,dq_part=p2((0,),(0,),sc,rows,qn,dn,st,st2,(P0,D0,m0),(own,),dq,last=True,back=back)
    grad_keys,grad_values=sum_parts(total,*late)
    grad_queries=(dq_own+swap(dq_part).astype(f32)).astype(bf16)
    return grad_queries,grad_keys,grad_values

def solution(mesh):
    spec=P_(AXES,None)
    return jax.shard_map(body,mesh=mesh,in_specs=(spec,spec,spec,spec,P_(AXES)),out_specs=(spec,spec,spec),check_vma=False)
```

```python
import functools
import jax, jax.numpy as jnp
from jax import lax
from jax.sharding import PartitionSpec as P_
from jax.experimental import pallas as pl
from jax.experimental.pallas import tpu as pltpu
DH=128; B=256; MR=528; H=8
C=float(1.0/DH**0.5*1.4426950408889634)
SC=float(1.0/DH**0.5)
NEG=-1e30
f32=jnp.float32; bf16=jnp.bfloat16
VM=pl.BlockSpec(memory_space=pltpu.VMEM)
SM=pl.BlockSpec(memory_space=pltpu.SMEM)
HBM=pl.BlockSpec(memory_space=pltpu.HBM)
SMALL=pl.CostEstimate(flops=1024,bytes_accessed=1024,transcendentals=0)
LARGE=pl.CostEstimate(flops=10**10,bytes_accessed=1024,transcendentals=0)
def dot(a,b): return jnp.dot(a,b,preferred_element_type=f32)
def hbm(x): return pltpu.with_memory_space_constraint(x,pltpu.HBM)
def vin(x): return pltpu.with_memory_space_constraint(x,pltpu.VMEM)
def vout(shape,dt): return pltpu.VMEM(shape,dt)
def loop(n,f,unroll=1):
    def body(i,c):
        f(i)
        return c
    lax.fori_loop(0,n,body,0,unroll=unroll)

def pack_kernel(ids,k,v,msg,row,xi,sem):
    copies=[pltpu.make_async_copy(ids,xi,sem.at[0]),
            pltpu.make_async_copy(k,msg.at[pl.ds(0,B)],sem.at[1]),
            pltpu.make_async_copy(v,msg.at[pl.ds(B,B)],sem.at[2])]
    for c in copies: c.start()
    for c in copies: c.wait()
    x=xi[...].astype(f32)
    msg[pl.ds(2*B,16),:]=jnp.concatenate([x,jnp.full((14,DH),-1.0,f32)],0).astype(bf16)
    r=jnp.concatenate([x[0:1],x[1:2]],1)
    col=jnp.broadcast_to(r,(8,B)).T[:,0:1]
    begin=jnp.sum(jnp.where(col<r,1.0,0.0),axis=0,keepdims=True)
    same=jnp.where(r==jnp.min(r),1.0,0.0)
    row[...]=jnp.concatenate([r,begin,same,jnp.zeros((5,B),f32)],0)
def pack(ids,k,v):
    return pl.pallas_call(pack_kernel,
      out_shape=(vout((MR,DH),bf16),vout((8,B),f32)),
      in_specs=[HBM]*3,out_specs=(VM,VM),name="pack",
      scratch_shapes=[pltpu.VMEM((B//DH,DH),jnp.int32),pltpu.SemaphoreType.DMA((3,))],cost_estimate=SMALL,
      compiler_params=pltpu.CompilerParams(vmem_limit_bytes=4*2**20))(*[hbm(a) for a in (ids.reshape(B//DH,DH),k,v)])

def classify(parity,steps,rows,kv,cls,cnt):
    lo=[jnp.min(r[0:1,:]) for r in rows]
    one=[jnp.min(r[2:3,:])>0.5 for r in rows]
    for n,s in enumerate(steps):
        ids=kv[n,pl.ds(2*B,16),:].astype(f32)[0:2]
        for b in range(2):
            t=2*n+b
            if s==0 and b==0:
                cls[t]=1; cnt[t]=0
            else:
                match=jnp.sum(jnp.where(ids==lo[b],1.0,0.0)).astype(jnp.int32)
                some=match>0
                if s==0: some=some&(parity==0)
                cls[t]=jnp.where(some,jnp.where((match==B)&one[b],2,1),0)
                cnt[t]=B-match
def bias_of(diag,rows,b,cnt):
    begin=jnp.where(b==0,rows[0][1:2],rows[1][1:2]); first=jnp.where(b==0,rows[0][2:3],rows[1][2:3])
    lb=jnp.where(first>0.5,cnt.astype(f32),1e9)
    u=lax.broadcasted_iota(jnp.int32,(B,B),0).astype(f32)
    if diag:
        lb=jnp.where(b==0,begin,lb)
        ub=jnp.where(b==0,lax.broadcasted_iota(jnp.int32,(1,B),1).astype(f32),1e9)
        return jnp.where((u>=lb)&(u<=ub),0.0,NEG)
    return jnp.where(u>=lb,0.0,NEG)

def p1_kernel(steps,first,*refs):
    n_kv=len(steps)
    it=iter(refs)
    sc=next(it); rows=[next(it),next(it)]
    if first: qd=[next(it) for _ in range(4)]
    else: qt,dt=next(it),next(it)
    kvs=[next(it) for _ in range(n_kv)]
    if not first: st_in=next(it)
    st=next(it); P=next(it); D=next(it); mj=next(it)
    if first: qt,dt,qn,dn=next(it),next(it),next(it),next(it)
    cls,cnt,bias=next(it),next(it),next(it)
    kv,sem=next(it),next(it)
    fetch=[pltpu.make_async_copy(kvs[n],kv.at[n],sem.at[2+n]) for n in range(n_kv)]
    for c in fetch: c.start()
    if first:
        qv,dv=next(it),next(it)
        copies=[pltpu.make_async_copy(qd[0],qv,sem.at[0]),pltpu.make_async_copy(qd[2],dv,sem.at[1])]
        for c in copies: c.start()
        def flip(b,q,d):
            for h in range(H):
                x=q[:,pl.ds(h*DH,DH)]; y=d[:,pl.ds(h*DH,DH)]
                qn[b*H+h]=x; dn[b*H+h]=y
                qt[b*H+h]=x.T; dt[b*H+h]=y.T
        flip(1,qd[1],qd[3])
        st[0]=jnp.full((2*H,B),NEG,f32)
        st[1]=jnp.zeros((2*H,B),f32)
        st[2]=jnp.zeros((2*H,B),f32)
        for c in fetch: c.wait()
        classify(sc[0],steps,rows,kv,cls,cnt)
        for c in copies: c.wait()
        flip(0,qv,dv)
    else:
        st[...]=st_in[...]
        for c in fetch: c.wait()
        classify(sc[0],steps,rows,kv,cls,cnt)
    def tile(t,masked):
        n=t//2; b=t%2
        if masked: bias[...]=bias_of(steps[0]==0,rows,b,cnt[t])
        K=kv[n,pl.ds(0,B),:]; V=kv[n,pl.ds(B,B),:]
        for h in range(H):
            i=b*H+h; j=t*H+h
            S=dot(K,qt[i])
            if masked: S=S+bias[...]
            at=pl.ds(i,1)
            old=st[0,at]
            mn=jnp.maximum(old,jnp.max(S,axis=0,keepdims=True))
            p=jnp.exp2(S*C-mn*C)
            dP=dot(V,dt[i])
            al=jnp.exp2((old-mn)*C)
            l=st[1,at]*al+jnp.sum(p,axis=0,keepdims=True)
            d=st[2,at]*al+jnp.sum(p*dP,axis=0,keepdims=True)
            st[0,at]=mn; st[1,at]=l; st[2,at]=d
            mj[pl.ds(j,1)]=mn
            P[j]=p.astype(bf16)
            D[j]=dP
    def pick(t):
        c=cls[t]
        @pl.when(c==1)
        def _(): tile(t,True)
        @pl.when(c==2)
        def _(): tile(t,False)
    loop(2*n_kv,pick)
def p1(steps,sc,rows,ops,kvs,st=None):
    n=len(steps); first=st is None
    outs=[vout((3,2*H,B),f32),vout((2*n*H,B,B),bf16),vout((2*n*H,B,B),f32),vout((2*n*H,B),f32)]
    if first: outs+=[vout((2*H,DH,B),bf16)]*2+[vout((2*H,B,DH),bf16)]*2
    ops=[hbm(ops[0]),vin(ops[1]),hbm(ops[2]),vin(ops[3])] if first else [vin(a) for a in ops]
    args=[*[vin(r) for r in rows],*ops,*[vin(a) for a in kvs]]+([] if first else [vin(st)])
    specs=[SM]+[VM]*len(args)
    if first: specs[3]=specs[5]=HBM
    return pl.pallas_call(functools.partial(p1_kernel,steps,first),
      out_shape=tuple(outs),
      in_specs=specs, out_specs=tuple([VM]*len(outs)),
      scratch_shapes=[pltpu.SMEM((2*n,),jnp.int32),pltpu.SMEM((2*n,),jnp.int32),pltpu.VMEM((B,B),f32),
        pltpu.VMEM((n,MR,DH),bf16),pltpu.SemaphoreType.DMA((2+n,))]+([pltpu.VMEM((B,H*DH),bf16)]*2 if first else []),
      cost_estimate=SMALL,compiler_params=pltpu.CompilerParams(vmem_limit_bytes=6*2**20),name="scores_"+"".join(map(str,steps)))(sc,*args)

def grad_tile(P,D,mj,j,L,i,kt,qn,dn,dq,acc):
    dk=jnp.zeros((B,DH),f32); dv=jnp.zeros((B,DH),f32)
    for h in range(H):
        fac=jnp.exp2(mj[pl.ds(j+h,1)]*C-L[0,pl.ds(i+h,1)])
        p=P[j+h].astype(f32)*fac
        g=(p*(D[j+h]-L[1,pl.ds(i+h,1)])).astype(bf16)
        dv=dv+dot(p.astype(bf16),dn[i+h])
        dk=dk+dot(g,qn[i+h])
        dq[i+h]+=dot(kt[...],g)
    acc[0]+=dk; acc[1]+=dv

def far_kernel(steps,sc,r0,r1,qn,dn,sta,stb,P,D,mj,k0,k1,g0,g1,dq,L,cls,cnt,acc,kv,kt,sem):
    kvs=(k0,k1)
    fetch=[pltpu.make_async_copy(kvs[n],kv.at[n],sem.at[n]) for n in range(2)]
    for c in fetch: c.start()
    dq[...]=jnp.zeros_like(dq)
    acc[...]=jnp.zeros_like(acc)
    swapped=lambda k: jnp.concatenate([stb[k,pl.ds(H,H)],stb[k,pl.ds(0,H)]],0)
    x=sta[0]; y=swapped(0)
    m=jnp.maximum(x,y)
    ax=jnp.exp2((x-m)*C); ay=jnp.exp2((y-m)*C)
    l=sta[1]*ax+swapped(1)*ay
    L[0]=m*C+jnp.log2(l)
    L[1]=(sta[2]*ax+swapped(2)*ay)/l
    for c in fetch: c.wait()
    remote_tiles(steps,sc,(r0,r1),qn,dn,L,P,D,mj,(g0,g1),dq,cls,cnt,acc,kv,kt)

def remote_tiles(steps,sc,rows,qn,dn,L,P,D,mj,gs,dq,cls,cnt,acc,kv,kt):
    classify(sc[0],steps,rows,kv,cls,cnt)
    for n in range(2): kt[n]=kv[n,pl.ds(0,B),:].T
    def pick(t):
        n=t//2; b=t%2
        @pl.when(cls[t]>0)
        def _(): grad_tile(P,D,mj,t*H,L,b*H,kt.at[n],qn,dn,dq,acc.at[n])
    loop(4,pick)
    for n in range(2):
        gs[n][pl.ds(0,B),:]=(acc[n,0]*SC).astype(bf16)
        gs[n][pl.ds(B,B),:]=acc[n,1].astype(bf16)

def near_kernel(steps,sc,r0,r1,qn,dn,L,P,D,mj,P0,D0,m0,k0,k1,own,dq_in,g0,g1,dq,part,acc0,cls,cnt,acc,kv,kt,sem):
    kvs=(k0,k1,own)
    fetch=[pltpu.make_async_copy(kvs[n],kv.at[n],sem.at[n]) for n in range(3)]
    for c in fetch: c.start()
    acc[...]=jnp.zeros_like(acc)
    acc0[...]=jnp.zeros_like(acc0)
    for c in fetch: c.wait()
    remote_tiles(steps,sc,(r0,r1),qn,dn,L,P,D,mj,(g0,g1),dq,cls,cnt,acc,kv,kt)
    @pl.when(cls[5]>0)
    def _():
        kt[2]=kv[2,pl.ds(0,B),:].T
        grad_tile(P0,D0,m0,H,L,H,kt.at[2],qn,dn,dq,acc0)
    for h in range(H): part[:,pl.ds(h*DH,DH)]=(dq[H+h]*SC).astype(bf16).T

def own_kernel(qn,dn,L,P0,D0,m0,own,dq_in,acc_in,b0,b1,out,total,dq,acc,kt):
    kt[...]=own[pl.ds(0,B),:].T
    acc[...]=acc_in[...]
    dq[...]=dq_in[pl.ds(0,H)]
    grad_tile(P0,D0,m0,0,L,0,kt,qn,dn,dq,acc)
    for h in range(H):
        at=pl.ds(h*DH,DH)
        out[:,at]=dq[h].T*SC
    for k,scale in ((0,SC),(1,1.0)):
        at=pl.ds(k*B,B)
        total[at,:]=acc[k]*scale+b0[at,:].astype(f32)+b1[at,:].astype(f32)

def params(mb): return pltpu.CompilerParams(vmem_limit_bytes=mb*2**20)
def work(n):
    return [pltpu.SMEM((2*n,),jnp.int32),pltpu.SMEM((2*n,),jnp.int32),pltpu.VMEM((2,2,B,DH),f32),
            pltpu.VMEM((n,MR,DH),bf16),pltpu.VMEM((n,DH,B),bf16),pltpu.SemaphoreType.DMA((n,))]
BLOCK=lambda: vout((2*B,DH),bf16)
def far_grads(steps,sc,rows,qn,dn,st,st2,pdm,kvs):
    args=[*rows,qn,dn,st,st2,*pdm,*kvs]
    return pl.pallas_call(functools.partial(far_kernel,steps),
      out_shape=(BLOCK(),BLOCK(),vout((2*H,DH,B),f32),vout((2,2*H,B),f32)),
      in_specs=[SM]+[VM]*len(args),out_specs=(VM,)*4,scratch_shapes=work(2),
      cost_estimate=SMALL,compiler_params=params(8),name="grads_far")(sc,*[vin(a) for a in args])
def near_grads(steps,sc,rows,qn,dn,L,pdm,pdm0,kvs,own,dq):
    args=[*rows,qn,dn,L,*pdm,*pdm0,*kvs,own,dq]
    return pl.pallas_call(functools.partial(near_kernel,(*steps,0)),
      out_shape=(BLOCK(),BLOCK(),vout((2*H,DH,B),f32),vout((B,H*DH),bf16),vout((2,B,DH),f32)),
      in_specs=[SM]+[VM]*len(args),out_specs=(VM,)*5,scratch_shapes=work(3),
      input_output_aliases={len(args):2},
      cost_estimate=LARGE,compiler_params=params(8),name="grads_near")(sc,*[vin(a) for a in args])
def own_grads(qn,dn,L,pdm0,own,dq,acc,back):
    args=[qn,dn,L,*pdm0,own,dq,acc,*back]
    return pl.pallas_call(own_kernel,
      out_shape=(vout((B,H*DH),f32),vout((2*B,DH),f32)),
      in_specs=[VM]*len(args),out_specs=(VM,VM),
      scratch_shapes=[pltpu.VMEM((H,DH,B),f32),pltpu.VMEM((2,B,DH),f32),pltpu.VMEM((DH,B),bf16)],
      cost_estimate=LARGE,compiler_params=params(8),name="grads_own")(*[vin(a) for a in args])

def finish_kernel(a,t,b,x,y,dq,dk,dv):
    dq[...]=(a[...]+b[...].astype(f32)).astype(bf16)
    s=t[...]+x[...].astype(f32)+y[...].astype(f32)
    dk[...]=s[0:B].astype(bf16)
    dv[...]=s[B:].astype(bf16)
def finish(*args):
    o=jax.ShapeDtypeStruct((B,DH),bf16)
    return pl.pallas_call(finish_kernel,out_shape=(jax.ShapeDtypeStruct((B,H*DH),bf16),o,o),
      in_specs=[VM]*5,out_specs=(VM,VM,VM),name="finish",cost_estimate=SMALL,
      compiler_params=params(4))(*[vin(a) for a in args])

AXES=("outer","inner")
def shift(x,by):
    n=lax.axis_size(AXES)
    return lax.ppermute(x,AXES,[(i,(i+by)%n) for i in range(n)])
def swap(x):
    n=lax.axis_size(AXES)
    return lax.ppermute(x,AXES,[(i,i^1) for i in range(n)])

def body(queries,key_rows,value_rows,grad_out,doc_ids):
    own,row_own=pack(doc_ids,key_rows,value_rows)
    got={s:shift(own,2*s) for s in (2,4,3,1)}
    row_other=swap(row_own); q_other=swap(queries); do_other=swap(grad_out)
    sc=(lax.axis_index("inner")%2).astype(jnp.int32).reshape(1)
    rows=(row_own,row_other)
    st,P0,D0,m0,qt,dt,qn,dn=p1((0,),sc,rows,(queries,q_other,grad_out,do_other),[own])
    own0=(P0,D0,m0)
    st,*near=p1((1,3),sc,rows,(qt,dt),(got[1],got[3]),st)
    st,*far=p1((4,2),sc,rows,(qt,dt),(got[4],got[2]),st)
    st2=swap(st)
    g4,g2,dq,lse=far_grads((4,2),sc,rows,qn,dn,st,st2,far,(got[4],got[2]))
    back=[shift(g4,-8),shift(g2,-4)]
    g1,g3,dq,part,acc=near_grads((1,3),sc,rows,qn,dn,lse,near,own0,(got[1],got[3]),own,dq)
    late=[shift(g1,-2),shift(g3,-6)]
    dq_own,total=own_grads(qn,dn,lse,own0,own,dq,acc,back)
    return finish(dq_own,total,swap(part),*late)

def solution(mesh):
    spec=P_(AXES,None)
    return jax.shard_map(body,mesh=mesh,in_specs=(spec,spec,spec,spec,P_(AXES)),out_specs=(spec,spec,spec),check_vma=False)
```

```python
import functools
import jax, jax.numpy as jnp
from jax import lax
from jax.sharding import PartitionSpec as P_
from jax.experimental import pallas as pl
from jax.experimental.pallas import tpu as pltpu
DH=128; B=256; MR=528; H=8
C=float(1.0/DH**0.5*1.4426950408889634)
SC=float(1.0/DH**0.5)
NEG=-1e30
f32=jnp.float32; bf16=jnp.bfloat16
VM=pl.BlockSpec(memory_space=pltpu.VMEM)
SM=pl.BlockSpec(memory_space=pltpu.SMEM)
HBM=pl.BlockSpec(memory_space=pltpu.HBM)
SMALL=pl.CostEstimate(flops=1024,bytes_accessed=1024,transcendentals=0)
LARGE=pl.CostEstimate(flops=10**10,bytes_accessed=1024,transcendentals=0)
def dot(a,b): return jnp.dot(a,b,preferred_element_type=f32)
def hbm(x): return pltpu.with_memory_space_constraint(x,pltpu.HBM)
def vin(x): return pltpu.with_memory_space_constraint(x,pltpu.VMEM)
def vout(shape,dt): return pltpu.VMEM(shape,dt)
def loop(n,f,unroll=1):
    def body(i,c):
        f(i)
        return c
    lax.fori_loop(0,n,body,0,unroll=unroll)

def pack_kernel(ids,k,v,msg,row,xi,sem):
    copies=[pltpu.make_async_copy(ids,xi,sem.at[0]),
            pltpu.make_async_copy(k,msg.at[pl.ds(0,B)],sem.at[1]),
            pltpu.make_async_copy(v,msg.at[pl.ds(B,B)],sem.at[2])]
    for c in copies: c.start()
    for c in copies: c.wait()
    x=xi[...].astype(f32)
    msg[pl.ds(2*B,16),:]=jnp.concatenate([x,jnp.full((14,DH),-1.0,f32)],0).astype(bf16)
    r=jnp.concatenate([x[0:1],x[1:2]],1)
    col=jnp.broadcast_to(r,(8,B)).T[:,0:1]
    begin=jnp.sum(jnp.where(col<r,1.0,0.0),axis=0,keepdims=True)
    same=jnp.where(r==jnp.min(r),1.0,0.0)
    row[...]=jnp.concatenate([r,begin,same,jnp.zeros((5,B),f32)],0)
def pack(ids,k,v):
    return pl.pallas_call(pack_kernel,
      out_shape=(vout((MR,DH),bf16),vout((8,B),f32)),
      in_specs=[HBM]*3,out_specs=(VM,VM),name="pack",
      scratch_shapes=[pltpu.VMEM((B//DH,DH),jnp.int32),pltpu.SemaphoreType.DMA((3,))],cost_estimate=SMALL,
      compiler_params=pltpu.CompilerParams(vmem_limit_bytes=4*2**20))(*[hbm(a) for a in (ids.reshape(B//DH,DH),k,v)])

def classify(parity,steps,rows,kv,cls,cnt):
    lo=[jnp.min(r[0:1,:]) for r in rows]
    one=[jnp.min(r[2:3,:])>0.5 for r in rows]
    for n,s in enumerate(steps):
        ids=kv[n,pl.ds(2*B,16),:].astype(f32)[0:2]
        for b in range(2):
            t=2*n+b
            if s==0 and b==0:
                cls[t]=1; cnt[t]=0
            else:
                match=jnp.sum(jnp.where(ids==lo[b],1.0,0.0)).astype(jnp.int32)
                some=match>0
                if s==0: some=some&(parity==0)
                cls[t]=jnp.where(some,jnp.where((match==B)&one[b],2,1),0)
                cnt[t]=B-match
def bias_of(diag,rows,b,cnt):
    begin=jnp.where(b==0,rows[0][1:2],rows[1][1:2]); first=jnp.where(b==0,rows[0][2:3],rows[1][2:3])
    lb=jnp.where(first>0.5,cnt.astype(f32),1e9)
    u=lax.broadcasted_iota(jnp.int32,(B,B),0).astype(f32)
    if diag:
        lb=jnp.where(b==0,begin,lb)
        ub=jnp.where(b==0,lax.broadcasted_iota(jnp.int32,(1,B),1).astype(f32),1e9)
        return jnp.where((u>=lb)&(u<=ub),0.0,NEG)
    return jnp.where(u>=lb,0.0,NEG)

def p1_kernel(steps,first,*refs):
    n_kv=len(steps)
    it=iter(refs)
    sc=next(it); rows=[next(it),next(it)]
    if first: qd=[next(it) for _ in range(4)]
    else: qt,dt=next(it),next(it)
    kvs=[next(it) for _ in range(n_kv)]
    if not first: st_in=next(it)
    st=next(it); P=next(it); D=next(it); mj=next(it)
    if first: qt,dt,qn,dn=next(it),next(it),next(it),next(it)
    cls,cnt,bias=next(it),next(it),next(it)
    kv,sem=next(it),next(it)
    fetch=[pltpu.make_async_copy(kvs[n],kv.at[n],sem.at[2+n]) for n in range(n_kv)]
    for c in fetch: c.start()
    if first:
        qv,dv=next(it),next(it)
        copies=[pltpu.make_async_copy(qd[0],qv,sem.at[0]),pltpu.make_async_copy(qd[2],dv,sem.at[1])]
        for c in copies: c.start()
        def flip(b,q,d):
            for h in range(H):
                x=q[:,pl.ds(h*DH,DH)]; y=d[:,pl.ds(h*DH,DH)]
                qn[b*H+h]=x; dn[b*H+h]=y
                qt[b*H+h]=x.T; dt[b*H+h]=y.T
        flip(1,qd[1],qd[3])
        st[0]=jnp.full((2*H,B),NEG,f32)
        st[1]=jnp.zeros((2*H,B),f32)
        st[2]=jnp.zeros((2*H,B),f32)
        for c in fetch: c.wait()
        classify(sc[0],steps,rows,kv,cls,cnt)
        for c in copies: c.wait()
        flip(0,qv,dv)
    else:
        st[...]=st_in[...]
        for c in fetch: c.wait()
        classify(sc[0],steps,rows,kv,cls,cnt)
    def tile(t,masked):
        n=t//2; b=t%2
        if masked: bias[...]=bias_of(steps[0]==0,rows,b,cnt[t])
        K=kv[n,pl.ds(0,B),:]; V=kv[n,pl.ds(B,B),:]
        for h in range(H):
            i=b*H+h; j=t*H+h
            S=dot(K,qt[i])
            if masked: S=S+bias[...]
            at=pl.ds(i,1)
            old=st[0,at]
            mn=jnp.maximum(old,jnp.max(S,axis=0,keepdims=True))
            p=jnp.exp2(S*C-mn*C)
            dP=dot(V,dt[i])
            al=jnp.exp2((old-mn)*C)
            l=st[1,at]*al+jnp.sum(p,axis=0,keepdims=True)
            d=st[2,at]*al+jnp.sum(p*dP,axis=0,keepdims=True)
            st[0,at]=mn; st[1,at]=l; st[2,at]=d
            mj[pl.ds(j,1)]=mn
            P[j]=p.astype(bf16)
            D[j]=dP
    def pick(t):
        c=cls[t]
        @pl.when(c==1)
        def _(): tile(t,True)
        @pl.when(c==2)
        def _(): tile(t,False)
    loop(2*n_kv,pick)
def p1(steps,sc,rows,ops,kvs,st=None):
    n=len(steps); first=st is None
    outs=[vout((3,2*H,B),f32),vout((2*n*H,B,B),bf16),vout((2*n*H,B,B),f32),vout((2*n*H,B),f32)]
    if first: outs+=[vout((2*H,DH,B),bf16)]*2+[vout((2*H,B,DH),bf16)]*2
    ops=[hbm(ops[0]),vin(ops[1]),hbm(ops[2]),vin(ops[3])] if first else [vin(a) for a in ops]
    args=[*[vin(r) for r in rows],*ops,*[vin(a) for a in kvs]]+([] if first else [vin(st)])
    specs=[SM]+[VM]*len(args)
    if first: specs[3]=specs[5]=HBM
    return pl.pallas_call(functools.partial(p1_kernel,steps,first),
      out_shape=tuple(outs),
      in_specs=specs, out_specs=tuple([VM]*len(outs)),
      scratch_shapes=[pltpu.SMEM((2*n,),jnp.int32),pltpu.SMEM((2*n,),jnp.int32),pltpu.VMEM((B,B),f32),
        pltpu.VMEM((n,MR,DH),bf16),pltpu.SemaphoreType.DMA((2+n,))]+([pltpu.VMEM((B,H*DH),bf16)]*2 if first else []),
      cost_estimate=SMALL,compiler_params=pltpu.CompilerParams(vmem_limit_bytes=6*2**20),name="scores_"+"".join(map(str,steps)))(sc,*args)

def grad_tile(P,D,mj,j,L,i,kt,qn,dn,dq,acc):
    dk=jnp.zeros((B,DH),f32); dv=jnp.zeros((B,DH),f32)
    for h in range(H):
        fac=jnp.exp2(mj[pl.ds(j+h,1)]*C-L[0,pl.ds(i+h,1)])
        p=P[j+h].astype(f32)*fac
        g=(p*(D[j+h]-L[1,pl.ds(i+h,1)])).astype(bf16)
        dv=dv+dot(p.astype(bf16),dn[i+h])
        dk=dk+dot(g,qn[i+h])
        dq[i+h]+=dot(kt[...],g)
    acc[0]+=dk; acc[1]+=dv

def far_kernel(steps,sc,r0,r1,qn,dn,sta,stb,P,D,mj,k0,k1,g0,g1,dq,L,cls,cnt,acc,kv,kt,sem):
    kvs=(k0,k1)
    fetch=[pltpu.make_async_copy(kvs[n],kv.at[n],sem.at[n]) for n in range(2)]
    for c in fetch: c.start()
    dq[...]=jnp.zeros_like(dq)
    acc[...]=jnp.zeros_like(acc)
    swapped=lambda k: jnp.concatenate([stb[k,pl.ds(H,H)],stb[k,pl.ds(0,H)]],0)
    x=sta[0]; y=swapped(0)
    m=jnp.maximum(x,y)
    ax=jnp.exp2((x-m)*C); ay=jnp.exp2((y-m)*C)
    l=sta[1]*ax+swapped(1)*ay
    L[0]=m*C+jnp.log2(l)
    L[1]=(sta[2]*ax+swapped(2)*ay)/l
    for c in fetch: c.wait()
    remote_tiles(steps,sc,(r0,r1),qn,dn,L,P,D,mj,(g0,g1),dq,cls,cnt,acc,kv,kt)

def remote_tiles(steps,sc,rows,qn,dn,L,P,D,mj,gs,dq,cls,cnt,acc,kv,kt):
    classify(sc[0],steps,rows,kv,cls,cnt)
    for n in range(2): kt[n]=kv[n,pl.ds(0,B),:].T
    def pick(t):
        n=t//2; b=t%2
        @pl.when(cls[t]>0)
        def _(): grad_tile(P,D,mj,t*H,L,b*H,kt.at[n],qn,dn,dq,acc.at[n])
    loop(4,pick)
    for n in range(2):
        gs[n][pl.ds(0,B),:]=(acc[n,0]*SC).astype(bf16)
        gs[n][pl.ds(B,B),:]=acc[n,1].astype(bf16)

def near_kernel(steps,sc,r0,r1,qn,dn,L,P,D,mj,P0,D0,m0,k0,k1,own,dq_in,g0,g1,dq,part,acc0,cls,cnt,acc,kv,kt,sem):
    kvs=(k0,k1,own)
    fetch=[pltpu.make_async_copy(kvs[n],kv.at[n],sem.at[n]) for n in range(3)]
    for c in fetch: c.start()
    acc[...]=jnp.zeros_like(acc)
    acc0[...]=jnp.zeros_like(acc0)
    for c in fetch: c.wait()
    remote_tiles(steps,sc,(r0,r1),qn,dn,L,P,D,mj,(g0,g1),dq,cls,cnt,acc,kv,kt)
    @pl.when(cls[5]>0)
    def _():
        kt[2]=kv[2,pl.ds(0,B),:].T
        grad_tile(P0,D0,m0,H,L,H,kt.at[2],qn,dn,dq,acc0)
    for h in range(H): part[:,pl.ds(h*DH,DH)]=(dq[H+h]*SC).astype(bf16).T

def own_kernel(qn,dn,L,P0,D0,m0,own,dq_in,acc_in,b0,b1,out,total,dq,acc,kt):
    kt[...]=own[pl.ds(0,B),:].T
    acc[...]=acc_in[...]
    dq[...]=dq_in[pl.ds(0,H)]
    grad_tile(P0,D0,m0,0,L,0,kt,qn,dn,dq,acc)
    for h in range(H):
        at=pl.ds(h*DH,DH)
        out[:,at]=dq[h].T*SC
    for k,scale in ((0,SC),(1,1.0)):
        at=pl.ds(k*B,B)
        total[at,:]=acc[k]*scale+b0[at,:].astype(f32)+b1[at,:].astype(f32)

def params(mb): return pltpu.CompilerParams(vmem_limit_bytes=mb*2**20)
def work(n):
    return [pltpu.SMEM((2*n,),jnp.int32),pltpu.SMEM((2*n,),jnp.int32),pltpu.VMEM((2,2,B,DH),f32),
            pltpu.VMEM((n,MR,DH),bf16),pltpu.VMEM((n,DH,B),bf16),pltpu.SemaphoreType.DMA((n,))]
BLOCK=lambda: vout((2*B,DH),bf16)
def far_grads(steps,sc,rows,qn,dn,st,st2,pdm,kvs):
    args=[*rows,qn,dn,st,st2,*pdm,*kvs]
    return pl.pallas_call(functools.partial(far_kernel,steps),
      out_shape=(BLOCK(),BLOCK(),vout((2*H,DH,B),f32),vout((2,2*H,B),f32)),
      in_specs=[SM]+[VM]*len(args),out_specs=(VM,)*4,scratch_shapes=work(2),
      cost_estimate=SMALL,compiler_params=params(8),name="grads_far")(sc,*[vin(a) for a in args])
def near_grads(steps,sc,rows,qn,dn,L,pdm,pdm0,kvs,own,dq):
    args=[*rows,qn,dn,L,*pdm,*pdm0,*kvs,own,dq]
    return pl.pallas_call(functools.partial(near_kernel,(*steps,0)),
      out_shape=(BLOCK(),BLOCK(),vout((2*H,DH,B),f32),vout((B,H*DH),bf16),vout((2,B,DH),f32)),
      in_specs=[SM]+[VM]*len(args),out_specs=(VM,)*5,scratch_shapes=work(3),
      input_output_aliases={len(args):2},
      cost_estimate=LARGE,compiler_params=params(8),name="grads_near")(sc,*[vin(a) for a in args])
def own_grads(qn,dn,L,pdm0,own,dq,acc,back):
    args=[qn,dn,L,*pdm0,own,dq,acc,*back]
    return pl.pallas_call(own_kernel,
      out_shape=(vout((B,H*DH),f32),vout((2*B,DH),f32)),
      in_specs=[VM]*len(args),out_specs=(VM,VM),
      scratch_shapes=[pltpu.VMEM((H,DH,B),f32),pltpu.VMEM((2,B,DH),f32),pltpu.VMEM((DH,B),bf16)],
      cost_estimate=LARGE,compiler_params=params(8),name="grads_own")(*[vin(a) for a in args])

def finish_kernel(a,t,b,x,y,dq,dk,dv):
    dq[...]=(a[...]+b[...].astype(f32)).astype(bf16)
    s=t[...]+x[...].astype(f32)+y[...].astype(f32)
    dk[...]=s[0:B].astype(bf16)
    dv[...]=s[B:].astype(bf16)
def finish(*args):
    o=jax.ShapeDtypeStruct((B,DH),bf16)
    return pl.pallas_call(finish_kernel,out_shape=(jax.ShapeDtypeStruct((B,H*DH),bf16),o,o),
      in_specs=[VM]*5,out_specs=(VM,VM,VM),name="finish",cost_estimate=SMALL,
      compiler_params=params(4))(*[vin(a) for a in args])

AXES=("outer","inner")
def shift(x,by):
    n=lax.axis_size(AXES)
    return lax.ppermute(x,AXES,[(i,(i+by)%n) for i in range(n)])
def swap(x):
    n=lax.axis_size(AXES)
    return lax.ppermute(x,AXES,[(i,i^1) for i in range(n)])

def body(queries,key_rows,value_rows,grad_out,doc_ids):
    own,row_own=pack(doc_ids,key_rows,value_rows)
    got={s:shift(own,2*s) for s in (2,4,3,1)}
    row_other=swap(row_own); q_other=swap(queries); do_other=swap(grad_out)
    sc=(lax.axis_index("inner")%2).astype(jnp.int32).reshape(1)
    rows=(row_own,row_other)
    st,P0,D0,m0,qt,dt,qn,dn=p1((0,),sc,rows,(queries,q_other,grad_out,do_other),[own])
    own0=(P0,D0,m0)
    st,*far=p1((2,4),sc,rows,(qt,dt),(got[2],got[4]),st)
    st,*near=p1((1,3),sc,rows,(qt,dt),(got[1],got[3]),st)
    st2=swap(st)
    g2,g4,dq,lse=far_grads((2,4),sc,rows,qn,dn,st,st2,far,(got[2],got[4]))
    back=[shift(g4,-8),shift(g2,-4)]
    g1,g3,dq,part,acc=near_grads((1,3),sc,rows,qn,dn,lse,near,own0,(got[1],got[3]),own,dq)
    late=[shift(g1,-2),shift(g3,-6)]
    dq_own,total=own_grads(qn,dn,lse,own0,own,dq,acc,back)
    return finish(dq_own,total,swap(part),*late)

def solution(mesh):
    spec=P_(AXES,None)
    return jax.shard_map(body,mesh=mesh,in_specs=(spec,spec,spec,spec,P_(AXES)),out_specs=(spec,spec,spec),check_vma=False)
```
